256 devices in a mesh: blk: 32 (over z, y_hi, core), group: 8 (over x, y_lo).
Axes of the slice: x: 4, y: 4 (y_hi: 2, y_lo: 2; y = y_hi * 2 + y_lo), z: 8, core: 2. Of those that a mesh axis runs over, the one named last changes fastest.
Arguments:
- quantized: bfloat16 [1024, 64, 128], P(('blk', 'group')), may hold values from -4 to 4
- block_scales: bfloat16 [1024, 64, 4], P(('blk', 'group')), may hold values from 0.25 to 4
- token_counts: int32 [1024], P(('blk', 'group')), may hold values from 8 to 64
- cluster_ids: int32 [1024], P(('blk', 'group')), may hold values from 0 to 255, as said below
Outputs:
- global_best: float32 [1024], P(('blk', 'group'))
- cluster_best: float32 [1024], P(('blk', 'group'))
The draws below stay inside these ranges and needn't reach their ends.
Inputs may be any that keep to these rules, and one draw needn't show every extreme that they name: `cluster_ids`: every cluster holds two or more documents; every id from 0 to the maximum is used.
All inputs are finite; a program needn't handle non-finite values.
Results may differ from the reference program's by a relative error of at most 0.00039.
Values may be sent and summed in bfloat16 or wider, within the bound.
A program may use at most 128 MiB of HBM per device.

```python
import math
import jax
import jax.numpy as jnp
from jax import lax

DIM = 128
TOKS = 64
DOC_DEV = 4
NB = 4
DOCS = 1024


def cluster_layout(key):
    first_key, second_key = jax.random.split(jax.random.fold_in(key, 23))
    doc_ranks = jax.random.permutation(first_key, DOCS).astype(jnp.int32)
    cluster_total = DOCS // 4
    pair_index = jnp.arange(DOCS // 2, dtype=jnp.int32)
    extra = jax.random.randint(second_key, (DOCS // 2,), 0, cluster_total, dtype=jnp.int32)
    pair_cluster = jnp.where(pair_index < cluster_total, pair_index, extra).astype(jnp.int32)
    return (doc_ranks, pair_cluster)


def draw_cluster_ids(key, part):
    doc_ranks, pair_cluster = cluster_layout(key)
    return pair_cluster[doc_ranks // 2]


def draw_token_counts(key, part):
    first_key, second_key = jax.random.split(jax.random.fold_in(key, 11))
    counts = jax.random.randint(first_key, (DOCS,), TOKS // 8, TOKS + 1, dtype=jnp.int32)
    chosen = jax.random.randint(second_key, (), 0, DOCS, dtype=jnp.int32)
    return counts.at[chosen].set(TOKS)


def draw_quantized(key, part):
    doc_ranks, pair_cluster = cluster_layout(key)
    holder = jnp.zeros((DOCS,), jnp.int32).at[doc_ranks].set(jnp.arange(DOCS, dtype=jnp.int32))
    pair_number = doc_ranks // 2
    copying = doc_ranks % 2 == 1
    within = pair_number % 2 == 0
    source_pair = jnp.where(within, pair_number, (pair_number + 1) % (DOCS // 2)).astype(jnp.int32)
    source_doc = holder[2 * source_pair]
    base_key, strength_key, order_key = jax.random.split(jax.random.fold_in(key, 37), 3)
    fresh_values = jnp.clip(jax.random.normal(base_key, (DOCS, TOKS, DIM), jnp.float32), -4.0, 4.0)
    strength = jax.random.uniform(strength_key, (DOCS,), jnp.float32, 0.35, 0.9)
    orders = jax.vmap(lambda one_key: jax.random.permutation(one_key, TOKS))(jax.random.split(order_key, DOCS)).astype(jnp.int32)
    source_tokens = fresh_values[source_doc[:, None], orders]
    remainder = jnp.sqrt(1.0 - strength * strength)
    blended = strength[:, None, None] * source_tokens + remainder[:, None, None] * fresh_values
    chosen_values = jnp.where(copying[:, None, None], blended, fresh_values)
    return jnp.clip(chosen_values, -4.0, 4.0).astype(jnp.bfloat16)


def levels(key, extent, cuts, least, high):
    def one(position, parts):
        heights = jax.random.uniform(jax.random.fold_in(jax.random.fold_in(key, 6), position), (parts,), jnp.float32, least / len(cuts), high / len(cuts))
        return jnp.repeat(jnp.exp(heights), extent[position] // parts).reshape((-1,) + (1,) * (len(extent) - position - 1))

    gain = one(*cuts[0])
    for cut in cuts[1:]:
        gain = gain * one(*cut)
    return gain


def setup_inputs(seed: int = 0) -> dict:
    splits = jax.random.split(jax.random.key(seed), 5)
    return {
        "quantized": draw_quantized(jax.random.fold_in(splits[4], 71), 0),
        "block_scales": jnp.clip(jnp.exp(math.log(4.0) - 2.7725887 * jax.random.uniform(splits[1], (DOCS, TOKS, NB), jnp.float32) ** levels(splits[1], (DOCS, TOKS, NB), ((0, 256),), -0.2, 0.2)), 0.25, 4.0).astype(jnp.bfloat16),
        "token_counts": draw_token_counts(jax.random.fold_in(splits[4], 71), 0),
        "cluster_ids": draw_cluster_ids(jax.random.fold_in(splits[4], 71), 0),
    }


NEG_FILL = -1e+30

def dequantize(quantized, block_scales):
    doc_count, tok_count, feature_width = quantized.shape
    blocks = block_scales.shape[2]
    grouped = quantized.reshape(doc_count, tok_count, blocks, feature_width // blocks).astype(jnp.float32)
    scaled = grouped * block_scales.astype(jnp.float32)[:, :, :, None]
    return scaled.reshape(doc_count, tok_count, feature_width).astype(jnp.bfloat16)

def chamfer_direct(queries, query_mask, query_count, key_values, key_counts, factor):
    key_docs, tok_count, feature_width = key_values.shape
    query_docs = query_mask.shape[0]
    products = lax.dot_general(queries, key_values.reshape(key_docs * tok_count, feature_width), (((1,), (1,)), ((), ())), preferred_element_type=jnp.float32)
    scores = products.reshape(query_docs, tok_count, key_docs, tok_count) * factor
    key_mask = lax.broadcasted_iota(jnp.int32, (key_docs, tok_count), 1) < key_counts[:, None]
    row_max = lax.optimization_barrier(jnp.max(jnp.where(key_mask[None, None, :, :], scores, NEG_FILL), axis=3))
    forward = lax.optimization_barrier(jnp.sum(jnp.where(query_mask[:, :, None], row_max, 0.0), axis=1)) / query_count[:, None]
    column_max = lax.optimization_barrier(jnp.max(jnp.where(query_mask[:, :, None, None], scores, NEG_FILL), axis=1))
    backward = lax.optimization_barrier(jnp.sum(jnp.where(key_mask[None, :, :], column_max, 0.0), axis=2)) / key_counts.astype(jnp.float32)[None, :]
    return 0.5 * (forward + backward)

def reference(quantized, block_scales, token_counts, cluster_ids):
    values = dequantize(quantized, block_scales)
    factor = 1.0 / math.sqrt(DIM)
    doc_index = jnp.arange(DOCS, dtype=jnp.int32)

    def one_block(block_index):
        first_doc = (block_index * DOC_DEV).astype(jnp.int32)
        query_docs = lax.dynamic_slice_in_dim(values, first_doc, DOC_DEV, 0)
        query_counts = lax.dynamic_slice_in_dim(token_counts, first_doc, DOC_DEV, 0)
        query_clusters = lax.dynamic_slice_in_dim(cluster_ids, first_doc, DOC_DEV, 0)
        query_ids = first_doc + jnp.arange(DOC_DEV, dtype=jnp.int32)
        query_mask = lax.broadcasted_iota(jnp.int32, (DOC_DEV, TOKS), 1) < query_counts[:, None]
        similar = chamfer_direct(query_docs.reshape(DOC_DEV * TOKS, DIM), query_mask, query_counts.astype(jnp.float32), values, token_counts, factor)
        distinct = doc_index[None, :] != query_ids[:, None]
        partner = distinct & (cluster_ids[None, :] == query_clusters[:, None])
        return (lax.optimization_barrier(jnp.max(jnp.where(distinct, similar, NEG_FILL), axis=1)), lax.optimization_barrier(jnp.max(jnp.where(partner, similar, NEG_FILL), axis=1)))
    global_best, cluster_best = lax.map(one_block, jnp.arange(DOCS // DOC_DEV, dtype=jnp.int32))
    return (global_best.reshape(DOCS), cluster_best.reshape(DOCS))
```

```python
import functools
import math

import jax
import jax.numpy as jnp
from jax import lax
from jax.experimental import pallas as pl
from jax.experimental.pallas import tpu as pltpu
from jax.sharding import PartitionSpec as P

NEG_FILL = -1e30
MESH = pl.DeviceIdType.MESH
TORUS = (4, 4, 8)

COLS = ((0, 0, 0), (0, 0, 1), (0, 0, 7), (0, 0, 2), (0, 0, 6), (0, 0, 3), (0, 0, 5), (0, 0, 4))
ROWS = (
    (0, 0, 0), (1, 0, 0), (0, 1, 0), (3, 3, 0), (1, 3, 0),
    (2, 0, 0), (0, 2, 0), (1, 2, 0), (2, 3, 0), (2, 2, 0),
)
N_COLS = len(COLS)
N_ROWS = len(ROWS)
SLOTS = 2 * N_COLS
DOCS = 4
TOKS = 64
DIM = 128
BODY = DOCS * TOKS
BLOCK = BODY + 16


def position():
    blk = lax.axis_index("blk")
    group = lax.axis_index("group")
    return group // 2, (blk // 2) % 2 * 2 + group % 2, blk // 4, blk % 2


def device_at(x, y, z, core):
    return ((z * 2 + y // 2) * 2 + core, x * 2 + y % 2)


def shifted(offset, other=0, sign=1):
    x, y, z, core = position()
    sx, sy, sz = TORUS
    return device_at(
        (x + sign * offset[0] + sx) % sx,
        (y + sign * offset[1] + sy) % sy,
        (z + sign * offset[2] + sz) % sz,
        (core + other) % 2,
    )


def partners():
    sends = set()
    for offset in COLS:
        minus = tuple(-v % n for v, n in zip(offset, TORUS))
        for other in (0, 1):
            sends.add((offset, other))
        sends.add((minus, 0))
    for offset in ROWS:
        minus = tuple(-v % n for v, n in zip(offset, TORUS))
        sends.add((offset, 0))
        sends.add((minus, 0))
    sends.discard(((0, 0, 0), 0))
    return sorted(sends)


def lanes(shape):
    return lax.broadcasted_iota(jnp.int32, shape, len(shape) - 1)


def sublanes(shape):
    return lax.broadcasted_iota(jnp.int32, shape, len(shape) - 2)


def roll_max(value, shifts, axis):
    for shift in shifts:
        value = jnp.maximum(value, pltpu.roll(value, shift, axis))
    return value


def roll_sum(value, shifts, axis):
    for shift in shifts:
        value = value + pltpu.roll(value, shift, axis)
    return value


def prepare(quantized, scales, counts, clusters, stage, block):
    tile = (TOKS, DIM)
    spread = (lanes((4, DIM)) // 32 == sublanes((4, DIM))).astype(jnp.bfloat16)
    token = sublanes(tile)
    for doc in range(DOCS):
        scale = lax.dot_general(
            scales[doc], spread, (((0,), (0,)), ((), ())), preferred_element_type=jnp.float32
        )
        value = quantized[doc].astype(jnp.float32) * scale
        value = value.astype(jnp.bfloat16).astype(jnp.float32)
        first = jnp.broadcast_to(value[0:1], tile)
        stage[pl.ds(doc, TOKS, stride=DOCS), :] = jnp.where(token < counts[doc], value, first)
    block[0:BODY, :] = stage[...].astype(jnp.bfloat16)
    doc_of_lane = lanes((16, DIM)) % DOCS
    meta = jnp.zeros((16, DIM), jnp.int32)
    for doc in range(DOCS):
        value = jnp.where(sublanes((16, DIM)) < 8, counts[doc], clusters[doc])
        meta = jnp.where(doc_of_lane == doc, value, meta)
    block[BODY:BLOCK, :] = meta.astype(jnp.float32).astype(jnp.bfloat16)


def half_scores(rows, half, col_ref):
    first = half * 8
    best = None
    tops = []
    for tile in range(8):
        keys = [
            col_ref[first : first + 8, (2 * tile + k) * 16 : (2 * tile + k + 1) * 16, :].reshape(
                128, DIM
            )
            for k in range(2)
        ]
        scores = lax.dot_general(
            rows,
            jnp.concatenate(keys, axis=0),
            (((1,), (1,)), ((), ())),
            preferred_element_type=jnp.float32,
        )
        for k in range(2):
            part = scores[:, 128 * k : 128 * (k + 1)]
            best = part if best is None else jnp.maximum(best, part)
            tops.append(jnp.max(part.reshape(BODY // 8, 8, 128), axis=0))
    return best, tops


def kernel(
    quantized, scales, counts, clusters,
    best_ref, cluster_ref,
    stage, col_ref, row_ref, key_count, key_cluster, over_keys, tops_ref, col_best, row_out, col_out, row_in, col_in,
    col_send, col_recv, core_send, core_recv, row_send, row_recv,
    col_out_send, col_in_recv, row_out_send, row_in_recv,
):
    barrier = pltpu.get_barrier_semaphore()
    around = partners()
    for offset, other in around:
        pl.semaphore_signal(
            barrier, 1, device_id=shifted(offset, other), device_id_type=MESH
        )
    own = col_ref.at[0]
    prepare(quantized, scales, counts, clusters, stage, own)
    row_ref[0] = col_ref[0]
    pl.semaphore_wait(barrier, len(around))

    def remote(source, target, send, recv, device):
        return pltpu.make_async_remote_copy(
            src_ref=source,
            dst_ref=target,
            send_sem=send,
            recv_sem=recv,
            device_id=device,
            device_id_type=MESH,
        )

    def to_sibling(k):
        return remote(
            col_ref.at[2 * k],
            col_ref.at[2 * k + 1],
            core_send.at[k],
            core_recv.at[k],
            shifted((0, 0, 0), 1),
        )

    col_copies = [
        remote(own, col_ref.at[2 * k], col_send.at[k], col_recv.at[k], shifted(COLS[k], 0, -1))
        if k
        else None
        for k in range(N_COLS)
    ]
    row_copies = [
        remote(own, row_ref.at[r], row_send.at[r], row_recv.at[r], shifted(ROWS[r], 0, -1))
        if r
        else None
        for r in range(N_ROWS)
    ]
    core_copies = [to_sibling(k) for k in range(N_COLS)]
    for copy in reversed(col_copies[1:]):
        copy.start()
    for copy in reversed(row_copies[1:]):
        copy.start()
    core_copies[0].start()
    for k in range(1, N_COLS):
        col_copies[k].wait_recv()
        core_copies[k].start()
    for k in range(N_COLS):
        core_copies[k].wait_recv()

    small = (8, DIM)
    lane = lanes(small)
    sub = sublanes(small)
    for half in range(2):
        meta = jnp.zeros((16, DIM), jnp.float32)
        for k in range(8):
            part = col_ref[8 * half + k, BODY:BLOCK, :].astype(jnp.float32)
            meta = jnp.where(lanes((16, DIM)) // 16 == k, part, meta)
        key_count[half] = meta[0:8]
        key_cluster[half] = meta[8:16]
    col_best[...] = jnp.full(col_best.shape, NEG_FILL, jnp.float32)

    factor = 0.5 / math.sqrt(DIM)
    key_token = lane % 16 // DOCS
    same_doc = (lane % DOCS) == (sub % DOCS)

    def row_step(r, state):
        @pl.when(r > 0)
        def _():
            remote(
                row_ref.at[0], row_ref.at[r], row_send.at[r], row_recv.at[r], shifted((0, 0, 0), 1)
            ).wait_recv()

        rows = row_ref[r, 0:BODY, :]
        meta = row_ref[r, BODY:BLOCK, :].astype(jnp.float32)
        pick = lanes((16, DIM)) == sublanes((16, DIM)) % DOCS
        chosen = jnp.sum(jnp.where(pick, meta, 0.0), axis=1, keepdims=True)
        row_count = jnp.broadcast_to(chosen[0:8], small)
        row_cluster = jnp.broadcast_to(chosen[8:16], small)
        best_row = jnp.full(small, NEG_FILL, jnp.float32)
        near_row = jnp.full(small, NEG_FILL, jnp.float32)
        for half in range(2):
            best, tops = half_scores(rows, half, col_ref)
            best = roll_max(best, (DIM - 4, DIM - 8), 1)
            forward = jnp.zeros(small, jnp.float32)
            for v in range(BODY // 8):
                token = (2 * v + sub // DOCS).astype(jnp.float32)
                forward = forward + jnp.where(token < row_count, best[8 * v : 8 * v + 8], 0.0)
            forward = roll_sum(forward, (4,), 0)
            backward = jnp.zeros(small, jnp.float32)
            for t in range(TOKS // 4):
                top = roll_max(tops[t], (4,), 0)
                token = (4 * t + key_token).astype(jnp.float32)
                backward = backward + jnp.where(token < key_count[half], top, 0.0)
            backward = roll_sum(backward, (DIM - 4, DIM - 8), 1)
            chamfer = factor * (forward / row_count + backward / key_count[half])
            distinct = lane % 16 < DOCS
            if half == 0:
                distinct = distinct & ~((lane // 16 == 0) & same_doc & (r == 0))
            partner = distinct & (key_cluster[half] == row_cluster)
            overall = jnp.where(distinct, chamfer, NEG_FILL)
            within = jnp.where(partner, chamfer, NEG_FILL)
            col_best[half, 0] = jnp.maximum(col_best[half, 0], overall)
            col_best[half, 1] = jnp.maximum(col_best[half, 1], within)
            best_row = jnp.maximum(best_row, overall)
            near_row = jnp.maximum(near_row, within)

        def by_lane(value):
            top = jnp.broadcast_to(jnp.max(value, axis=1, keepdims=True), small)
            return roll_max(jnp.where(same_doc, top, NEG_FILL), (1, 2), 0)

        row_out[r] = jnp.where(sub < 4, by_lane(best_row), by_lane(near_row))
        return state

    lax.fori_loop(0, N_ROWS, row_step, 0)

    for half in range(2):
        overall = roll_max(col_best[half, 0], (4, 2, 1), 0)
        within = roll_max(col_best[half, 1], (4, 2, 1), 0)
        col_out[half] = jnp.where(sub < 4, overall, within)

    row_outs = [
        remote(
            row_out.at[r], row_in.at[r], row_out_send.at[r], row_in_recv.at[r], shifted(ROWS[r])
        )
        for r in range(1, N_ROWS)
    ]
    col_outs = [
        remote(
            col_out.at[slot // 8],
            col_in.at[slot],
            col_out_send.at[slot],
            col_in_recv.at[slot],
            shifted(COLS[slot // 2], slot % 2),
        )
        for slot in range(1, SLOTS)
    ]
    for copy in row_outs + col_outs:
        copy.start()
    for k in range(1, N_COLS):
        col_copies[k].wait_send()
    for r in range(1, N_ROWS):
        row_copies[r].wait_send()
    for k in range(N_COLS):
        core_copies[k].wait_send()
    for copy in row_outs + col_outs:
        copy.wait_send()

    total = jnp.where(lane // 16 == 0, col_out[0], NEG_FILL)
    for slot in range(1, SLOTS):
        col_outs[slot - 1].wait_recv()
        total = jnp.maximum(total, jnp.where(lane // 16 == slot % 8, col_in[slot], NEG_FILL))
    total = roll_max(total, (16, 32, 64), 1)
    total = jnp.maximum(total, row_out[0])
    for r in range(1, N_ROWS):
        row_outs[r - 1].wait_recv()
        total = jnp.maximum(total, row_in[r])
    best_ref[...] = total[0:1, 0:DOCS]
    cluster_ref[...] = total[4:5, 0:DOCS]


def shards(quantized, block_scales, token_counts, cluster_ids):
    vmem = pl.BlockSpec(memory_space=pltpu.VMEM)
    smem = pl.BlockSpec(memory_space=pltpu.SMEM)
    scores = pl.pallas_call(
        kernel,
        out_shape=(
            jax.ShapeDtypeStruct((1, DOCS), jnp.float32),
            jax.ShapeDtypeStruct((1, DOCS), jnp.float32),
        ),
        in_specs=[vmem, vmem, smem, smem],
        out_specs=(vmem, vmem),
        scratch_shapes=[
            pltpu.VMEM((BODY, DIM), jnp.float32),
            pltpu.VMEM((SLOTS, BLOCK, DIM), jnp.bfloat16),
            pltpu.VMEM((N_ROWS, BLOCK, DIM), jnp.bfloat16),
            pltpu.VMEM((2, 8, DIM), jnp.float32),
            pltpu.VMEM((2, 8, DIM), jnp.float32),
            pltpu.VMEM((BODY, DIM), jnp.float32),
            pltpu.VMEM((TOKS // 4, 8, DIM), jnp.float32),
            pltpu.VMEM((2, 2, 8, DIM), jnp.float32),
            pltpu.VMEM((N_ROWS, 8, DIM), jnp.float32),
            pltpu.VMEM((2, 8, DIM), jnp.float32),
            pltpu.VMEM((N_ROWS, 8, DIM), jnp.float32),
            pltpu.VMEM((SLOTS, 8, DIM), jnp.float32),
            pltpu.SemaphoreType.DMA((N_COLS,)),
            pltpu.SemaphoreType.DMA((N_COLS,)),
            pltpu.SemaphoreType.DMA((N_COLS,)),
            pltpu.SemaphoreType.DMA((N_COLS,)),
            pltpu.SemaphoreType.DMA((N_ROWS,)),
            pltpu.SemaphoreType.DMA((N_ROWS,)),
            pltpu.SemaphoreType.DMA((SLOTS,)),
            pltpu.SemaphoreType.DMA((SLOTS,)),
            pltpu.SemaphoreType.DMA((N_ROWS,)),
            pltpu.SemaphoreType.DMA((N_ROWS,)),
        ],
        compiler_params=pltpu.CompilerParams(
            collective_id=0, has_side_effects=True, vmem_limit_bytes=40 << 20
        ),
    )(quantized, jnp.swapaxes(block_scales, 1, 2), token_counts, cluster_ids)
    return scores[0].reshape(DOCS), scores[1].reshape(DOCS)


def solution(mesh):
    placed = (
        P(("blk", "group"), None, None),
        P(("blk", "group"), None, None),
        P(("blk", "group")),
        P(("blk", "group")),
    )
    return jax.shard_map(
        shards,
        mesh=mesh,
        in_specs=placed,
        out_specs=(P(("blk", "group")), P(("blk", "group"))),
        check_vma=False,
    )
```

```python
import functools
import math

import jax
import jax.numpy as jnp
from jax import lax
from jax.experimental import pallas as pl
from jax.experimental.pallas import tpu as pltpu
from jax.sharding import PartitionSpec as P

NEG_FILL = -1e30
MESH = pl.DeviceIdType.MESH
TORUS = (4, 4, 8)

COLS = ((0, 0, 0), (0, 0, 1), (0, 0, 7), (0, 0, 2), (0, 0, 6), (0, 0, 3), (0, 0, 5), (0, 0, 4))
ROWS = (
    (0, 0, 0), (1, 0, 0), (0, 1, 0), (3, 3, 0), (3, 1, 0),
    (2, 0, 0), (0, 2, 0), (1, 2, 0), (2, 3, 0), (2, 2, 0),
)
N_COLS = len(COLS)
N_ROWS = len(ROWS)
SLOTS = 2 * N_COLS
DOCS = 4
TOKS = 64
DIM = 128
BODY = DOCS * TOKS
BLOCK = BODY + 16
CUT = 144
EARLY = 3


def position():
    blk = lax.axis_index("blk")
    group = lax.axis_index("group")
    return group >> 1, (blk & 2) | (group & 1), blk >> 2, blk & 1


def device_at(x, y, z, core):
    return ((z << 2) | (y & 2) | core, (x << 1) | (y & 1))


def shifted(offset, other=0, sign=1):
    x, y, z, core = position()
    step = tuple(sign * v % n for v, n in zip(offset, TORUS))
    return device_at(
        (x + step[0]) & (TORUS[0] - 1) if step[0] else x,
        (y + step[1]) & (TORUS[1] - 1) if step[1] else y,
        (z + step[2]) & (TORUS[2] - 1) if step[2] else z,
        core ^ other if other else core,
    )


def partners():
    sends = set()
    for offset in COLS:
        minus = tuple(-v % n for v, n in zip(offset, TORUS))
        for other in (0, 1):
            sends.add((offset, other))
        sends.add((minus, 0))
    for offset in ROWS:
        minus = tuple(-v % n for v, n in zip(offset, TORUS))
        sends.add((offset, 0))
        sends.add((minus, 0))
    sends.discard(((0, 0, 0), 0))
    return sorted(sends)


def lanes(shape):
    return lax.broadcasted_iota(jnp.int32, shape, len(shape) - 1)


def sublanes(shape):
    return lax.broadcasted_iota(jnp.int32, shape, len(shape) - 2)


def roll_max(value, shifts, axis):
    for shift in shifts:
        value = jnp.maximum(value, pltpu.roll(value, shift, axis))
    return value


def roll_sum(value, shifts, axis):
    for shift in shifts:
        value = value + pltpu.roll(value, shift, axis)
    return value


def prepare(quantized, scales, counts, clusters, stage, block):
    tile = (TOKS, DIM)
    spread = (lanes((4, DIM)) // 32 == sublanes((4, DIM))).astype(jnp.bfloat16)
    token = sublanes(tile)
    for doc in range(DOCS):
        scale = lax.dot_general(
            scales[doc], spread, (((0,), (0,)), ((), ())), preferred_element_type=jnp.float32
        )
        value = quantized[doc].astype(jnp.float32) * scale
        value = value.astype(jnp.bfloat16).astype(jnp.float32)
        first = jnp.broadcast_to(value[0:1], tile)
        stage[pl.ds(doc, TOKS, stride=DOCS), :] = jnp.where(token < counts[doc], value, first)
    block[0:BODY, :] = stage[...].astype(jnp.bfloat16)
    doc_of_lane = lanes((16, DIM)) % DOCS
    meta = jnp.zeros((16, DIM), jnp.int32)
    for doc in range(DOCS):
        value = jnp.where(sublanes((16, DIM)) < 8, counts[doc], clusters[doc])
        meta = jnp.where(doc_of_lane == doc, value, meta)
    block[BODY:BLOCK, :] = meta.astype(jnp.float32).astype(jnp.bfloat16)


def half_scores(rows, half, col_ref):
    first = half * 8
    blocks = rows.shape[0] // BODY
    best = None
    tops = [[] for _ in range(blocks)]
    for tile in range(8):
        keys = [
            col_ref[first : first + 8, (2 * tile + k) * 16 : (2 * tile + k + 1) * 16, :].reshape(
                128, DIM
            )
            for k in range(2)
        ]
        scores = lax.dot_general(
            rows,
            jnp.concatenate(keys, axis=0),
            (((1,), (1,)), ((), ())),
            preferred_element_type=jnp.float32,
        )
        for k in range(2):
            part = scores[:, 128 * k : 128 * (k + 1)]
            best = part if best is None else jnp.maximum(best, part)
            for q in range(blocks):
                block = part[BODY * q : BODY * (q + 1)]
                tops[q].append(jnp.max(block.reshape(BODY // 8, 8, 128), axis=0))
    return [best[BODY * q : BODY * (q + 1)] for q in range(blocks)], tops


def row_owner(r):
    x, y, z, core = position()
    xs = sum(offset[0] * 4**k for k, offset in enumerate(ROWS))
    ys = sum(offset[1] * 4**k for k, offset in enumerate(ROWS))
    return device_at((x + (xs >> (2 * r))) & 3, (y + (ys >> (2 * r))) & 3, z, core)


def kernel(
    quantized_hbm, scales_hbm, counts_hbm, clusters_hbm,
    best_ref, cluster_ref,
    quantized, scales, counts, clusters, load_sem,
    stage, col_ref, row_ref, key_count, key_cluster, row_side, row_best, col_best, row_out, col_out, row_in, col_in,
    col_send, col_recv, core_send, core_recv, row_send, row_recv,
    col_out_send, col_in_recv, row_out_send, row_in_recv,
):
    loads = [
        pltpu.make_async_copy(source, target, load_sem.at[k])
        for k, (source, target) in enumerate(
            (
                (counts_hbm, counts),
                (clusters_hbm, clusters),
                (scales_hbm, scales),
                (quantized_hbm, quantized),
            )
        )
    ]
    for load in loads:
        load.start()
    barrier = pltpu.get_barrier_semaphore()
    around = partners()
    for offset, other in around:
        pl.semaphore_signal(barrier, 1, device_id=shifted(offset, other), device_id_type=MESH)
    for load in loads:
        load.wait()
    own = col_ref.at[0]
    prepare(quantized, scales, counts, clusters, stage, own)
    row_ref[0] = col_ref[0]
    col_best[...] = jnp.full(col_best.shape, NEG_FILL, jnp.float32)
    pl.semaphore_wait(barrier, len(around))

    def remote(source, target, send, recv, device):
        return pltpu.make_async_remote_copy(
            src_ref=source,
            dst_ref=target,
            send_sem=send,
            recv_sem=recv,
            device_id=device,
            device_id_type=MESH,
        )

    def along(k, source, target, part, device):
        source, target = col_ref.at[2 * source], col_ref.at[2 * target]
        if part is not None:
            source, target = source.at[part[0] : part[1]], target.at[part[0] : part[1]]
        return remote(source, target, col_send.at[k], col_recv.at[k], device)

    col_copies = [
        along(0, 4, 7, (CUT, BLOCK), shifted(COLS[3])),
        along(1, 0, 1, None, shifted(COLS[2])),
        along(2, 0, 2, None, shifted(COLS[1])),
        along(3, 0, 3, None, shifted(COLS[4])),
        along(4, 0, 4, None, shifted(COLS[3])),
        along(5, 3, 5, None, shifted(COLS[2])),
        along(6, 4, 6, None, shifted(COLS[1])),
        along(7, 3, 7, (0, CUT), shifted(COLS[4])),
    ]
    core_copies = [
        remote(
            col_ref.at[2 * k],
            col_ref.at[2 * k + 1],
            core_send.at[k],
            core_recv.at[k],
            shifted((0, 0, 0), 1),
        )
        for k in range(N_COLS)
    ]
    row_copies = [
        remote(own, row_ref.at[r], row_send.at[r], row_recv.at[r], shifted(ROWS[r], 0, -1))
        for r in range(1, N_ROWS)
    ]
    for k in (3, 4, 1, 2):
        col_copies[k].start()
    core_copies[0].start()
    row_waves = ((1, 2, 3), (4, 5, 6), (7, 8, 9))
    for k, wave in enumerate(row_waves):
        for r in row_waves[k - 1] if k else ():
            row_copies[r - 1].wait_send()
        for r in wave:
            row_copies[r - 1].start()
    col_copies[3].wait_recv()
    col_copies[5].start()
    col_copies[7].start()
    col_copies[4].wait_recv()
    col_copies[6].start()
    col_copies[0].start()
    core_copies[3].start()
    for k in (1, 2):
        col_copies[k].wait_recv()
        core_copies[k].start()
    core_copies[4].start()

    small = (8, DIM)
    lane = lanes(small)
    sub = sublanes(small)
    factor = 0.5 / math.sqrt(DIM)
    same_doc = (lane % DOCS) == (sub % DOCS)

    def read_meta(half):
        for k in range(4 * half, 4 * half + 4):
            core_copies[k].wait_recv()
        meta = jnp.zeros((16, DIM), jnp.float32)
        for k in range(8):
            part = col_ref[8 * half + k, BODY:BLOCK, :].astype(jnp.float32)
            meta = jnp.where(lanes((16, DIM)) // 16 == k, part, meta)
        key_count[half] = meta[0:8]
        key_cluster[half] = meta[8:16]

    def row_meta(r):
        meta = row_ref[r, BODY:BLOCK, :].astype(jnp.float32)
        pick = lanes((16, DIM)) == sublanes((16, DIM)) % DOCS
        chosen = jnp.sum(jnp.where(pick, meta, 0.0), axis=1, keepdims=True)
        row_side[r, 0] = jnp.broadcast_to(chosen[0:8], small)
        row_side[r, 1] = jnp.broadcast_to(chosen[8:16], small)

    def pair_unit(p, half):
        rows = row_ref[pl.ds(2 * p, 2), 0:BODY, :].reshape(2 * BODY, DIM)
        bests, all_tops = half_scores(rows, half, col_ref)
        found = []
        for q in range(2):
            r = 2 * p + q
            row_count, row_cluster = row_side[r, 0], row_side[r, 1]
            best = roll_max(bests[q], (DIM - 4, DIM - 8), 1)
            forward = roll_sum(jnp.sum(best.reshape(BODY // 8, 8, DIM), axis=0), (4,), 0)
            start = jnp.where(sub < 4, best[0:8], pltpu.roll(best[0:8], 4, 0))
            forward = forward - (TOKS - row_count) * start
            tops = [roll_max(top, (4,), 0) for top in all_tops[q]]
            backward = roll_sum(functools.reduce(jnp.add, tops), (DIM - 4, DIM - 8), 1)
            backward = backward - (TOKS - key_count[half]) * tops[0]
            chamfer = factor * (forward / row_count + backward / key_count[half])
            distinct = lane % 16 < DOCS
            if half == 0:
                distinct = distinct & ~((lane // 16 == 0) & same_doc & (r == 0))
            partner = distinct & (key_cluster[half] == row_cluster)
            found.append((jnp.where(distinct, chamfer, NEG_FILL), jnp.where(partner, chamfer, NEG_FILL)))
        for side in range(2):
            top = jnp.maximum(found[0][side], found[1][side])
            col_best[half, side] = jnp.maximum(col_best[half, side], top)
        return found

    def row_copy(r):
        return remote(row_ref.at[0], row_ref.at[r], row_send.at[r], row_recv.at[r], row_owner(r))

    def row_result(r):
        return remote(
            row_out.at[r], row_in.at[r], row_out_send.at[r], row_in_recv.at[r], row_owner(r)
        )

    def first_half(p, state):
        @pl.when(p > 0)
        def _():
            row_copy(2 * p).wait_recv()

        row_copy(2 * p + 1).wait_recv()
        for q in range(2):
            row_meta(2 * p + q)
        for q, found in enumerate(pair_unit(p, 0)):
            row_best[2 * p + q, 0] = found[0]
            row_best[2 * p + q, 1] = found[1]
        return state

    def by_lane(value):
        top = jnp.broadcast_to(jnp.max(value, axis=1, keepdims=True), small)
        return roll_max(jnp.where(same_doc, top, NEG_FILL), (1, 2), 0)

    def second_half(p, state):
        for q, (overall, within) in enumerate(pair_unit(p, 1)):
            r = 2 * p + q
            overall = by_lane(jnp.maximum(overall, row_best[r, 0]))
            within = by_lane(jnp.maximum(within, row_best[r, 1]))
            row_out[r] = jnp.where(sub < 4, overall, within)

        @pl.when(p > 0)
        def _():
            row_result(2 * p).start()

        row_result(2 * p + 1).start()
        return state

    col_outs = [
        remote(
            col_out.at[slot // 8],
            col_in.at[slot],
            col_out_send.at[slot],
            col_in_recv.at[slot],
            shifted(COLS[slot // 2], slot % 2),
        )
        for slot in range(SLOTS)
    ]

    def return_cols(half):
        overall = roll_max(col_best[half, 0], (4, 2, 1), 0)
        within = roll_max(col_best[half, 1], (4, 2, 1), 0)
        col_out[half] = jnp.where(sub < 4, overall, within)
        for slot in range(max(1, 8 * half), 8 * half + 8):
            col_outs[slot].start()

    read_meta(0)
    lax.fori_loop(0, EARLY, first_half, 0)
    for k in (5, 6):
        col_copies[k].wait_recv()
        core_copies[k].start()
    col_copies[7].wait_recv()
    col_copies[0].wait_recv()
    core_copies[7].start()
    lax.fori_loop(EARLY, N_ROWS // 2, first_half, 0)
    return_cols(0)
    read_meta(1)
    lax.fori_loop(0, N_ROWS // 2, second_half, 0)
    return_cols(1)

    for copy in col_copies + [row_copies[r - 1] for r in row_waves[-1]] + core_copies:
        copy.wait_send()
    total = jnp.where(lane // 16 == 0, col_out[0], NEG_FILL)
    for slot in range(1, SLOTS):
        col_outs[slot].wait_recv()
        total = jnp.maximum(total, jnp.where(lane // 16 == slot % 8, col_in[slot], NEG_FILL))
    total = roll_max(total, (16, 32, 64), 1)
    total = jnp.maximum(total, row_out[0])
    for r in range(1, N_ROWS):
        row_result(r).wait_recv()
        total = jnp.maximum(total, row_in[r])
    best_ref[...] = total[0:1, 0:DOCS]
    cluster_ref[...] = total[4:5, 0:DOCS]
    for slot in range(1, SLOTS):
        col_outs[slot].wait_send()
    for r in range(1, N_ROWS):
        row_result(r).wait_send()


def shards(quantized, block_scales, token_counts, cluster_ids):
    vmem = pl.BlockSpec(memory_space=pltpu.VMEM)
    hbm = pl.BlockSpec(memory_space=pltpu.HBM)
    scores = pl.pallas_call(
        kernel,
        out_shape=(
            jax.ShapeDtypeStruct((1, DOCS), jnp.float32),
            jax.ShapeDtypeStruct((1, DOCS), jnp.float32),
        ),
        in_specs=[hbm] * 4,
        out_specs=(vmem, vmem),
        scratch_shapes=[
            pltpu.VMEM((DOCS, TOKS, DIM), jnp.bfloat16),
            pltpu.VMEM((DOCS, 4, TOKS), jnp.bfloat16),
            pltpu.SMEM((DOCS,), jnp.int32),
            pltpu.SMEM((DOCS,), jnp.int32),
            pltpu.SemaphoreType.DMA((4,)),
            pltpu.VMEM((BODY, DIM), jnp.float32),
            pltpu.VMEM((SLOTS, BLOCK, DIM), jnp.bfloat16),
            pltpu.VMEM((N_ROWS, BLOCK, DIM), jnp.bfloat16),
            pltpu.VMEM((2, 8, DIM), jnp.float32),
            pltpu.VMEM((2, 8, DIM), jnp.float32),
            pltpu.VMEM((N_ROWS, 2, 8, DIM), jnp.float32),
            pltpu.VMEM((N_ROWS, 2, 8, DIM), jnp.float32),
            pltpu.VMEM((2, 2, 8, DIM), jnp.float32),
            pltpu.VMEM((N_ROWS, 8, DIM), jnp.float32),
            pltpu.VMEM((2, 8, DIM), jnp.float32),
            pltpu.VMEM((N_ROWS, 8, DIM), jnp.float32),
            pltpu.VMEM((SLOTS, 8, DIM), jnp.float32),
            pltpu.SemaphoreType.DMA((N_COLS,)),
            pltpu.SemaphoreType.DMA((N_COLS,)),
            pltpu.SemaphoreType.DMA((N_COLS,)),
            pltpu.SemaphoreType.DMA((N_COLS,)),
            pltpu.SemaphoreType.DMA((N_ROWS,)),
            pltpu.SemaphoreType.DMA((N_ROWS,)),
            pltpu.SemaphoreType.DMA((SLOTS,)),
            pltpu.SemaphoreType.DMA((SLOTS,)),
            pltpu.SemaphoreType.DMA((N_ROWS,)),
            pltpu.SemaphoreType.DMA((N_ROWS,)),
        ],
        compiler_params=pltpu.CompilerParams(
            collective_id=0, has_side_effects=True, vmem_limit_bytes=63 << 20
        ),
    )(quantized, jnp.swapaxes(block_scales, 1, 2), token_counts, cluster_ids)
    return scores[0].reshape(DOCS), scores[1].reshape(DOCS)


def solution(mesh):
    placed = (
        P(("blk", "group"), None, None),
        P(("blk", "group"), None, None),
        P(("blk", "group")),
        P(("blk", "group")),
    )
    return jax.shard_map(
        shards,
        mesh=mesh,
        in_specs=placed,
        out_specs=(P(("blk", "group")), P(("blk", "group"))),
        check_vma=False,
    )
```

```python
import functools
import math

import jax
import jax.numpy as jnp
from jax import lax
from jax.experimental import pallas as pl
from jax.experimental.pallas import tpu as pltpu
from jax.sharding import PartitionSpec as P

NEG_FILL = -1e30
MESH = pl.DeviceIdType.MESH
TORUS = (4, 4, 8)

COLS = ((0, 0, 0), (0, 0, 1), (0, 0, 7), (0, 0, 2), (0, 0, 6), (0, 0, 3), (0, 0, 5), (0, 0, 4))
ROWS = (
    (0, 0, 0), (1, 0, 0), (0, 1, 0), (3, 3, 0), (3, 1, 0),
    (2, 0, 0), (0, 2, 0), (1, 2, 0), (2, 3, 0), (2, 2, 0),
)
N_COLS = len(COLS)
N_ROWS = len(ROWS)
SLOTS = 2 * N_COLS
DOCS = 4
TOKS = 64
DIM = 128
BODY = DOCS * TOKS
BLOCK = BODY + 16
CUT = 144
EARLY = 4


def position():
    blk = lax.axis_index("blk")
    group = lax.axis_index("group")
    return group >> 1, (blk & 2) | (group & 1), blk >> 2, blk & 1


def device_at(x, y, z, core):
    return ((z << 2) | (y & 2) | core, (x << 1) | (y & 1))


def shifted(offset, other=0, sign=1):
    x, y, z, core = position()
    step = tuple(sign * v % n for v, n in zip(offset, TORUS))
    return device_at(
        (x + step[0]) & (TORUS[0] - 1) if step[0] else x,
        (y + step[1]) & (TORUS[1] - 1) if step[1] else y,
        (z + step[2]) & (TORUS[2] - 1) if step[2] else z,
        core ^ other if other else core,
    )


def partners():
    sends = set()
    for offset in COLS:
        minus = tuple(-v % n for v, n in zip(offset, TORUS))
        for other in (0, 1):
            sends.add((offset, other))
        sends.add((minus, 0))
    for offset in ROWS:
        minus = tuple(-v % n for v, n in zip(offset, TORUS))
        sends.add((offset, 0))
        sends.add((minus, 0))
    sends.discard(((0, 0, 0), 0))
    return sorted(sends)


def lanes(shape):
    return lax.broadcasted_iota(jnp.int32, shape, len(shape) - 1)


def sublanes(shape):
    return lax.broadcasted_iota(jnp.int32, shape, len(shape) - 2)


def roll_max(value, shifts, axis):
    for shift in shifts:
        value = jnp.maximum(value, pltpu.roll(value, shift, axis))
    return value


def roll_sum(value, shifts, axis):
    for shift in shifts:
        value = value + pltpu.roll(value, shift, axis)
    return value


def prepare(quantized, scales, counts, clusters, stage, block):
    tile = (TOKS, DIM)
    spread = (lanes((4, DIM)) // 32 == sublanes((4, DIM))).astype(jnp.bfloat16)
    token = sublanes(tile)
    for doc in range(DOCS):
        scale = lax.dot_general(
            scales[doc], spread, (((0,), (0,)), ((), ())), preferred_element_type=jnp.float32
        )
        value = quantized[doc].astype(jnp.float32) * scale
        value = value.astype(jnp.bfloat16).astype(jnp.float32)
        first = jnp.broadcast_to(value[0:1], tile)
        stage[pl.ds(doc, TOKS, stride=DOCS), :] = jnp.where(token < counts[doc], value, first)
    block[0:BODY, :] = stage[...].astype(jnp.bfloat16)
    doc_of_lane = lanes((16, DIM)) % DOCS
    meta = jnp.zeros((16, DIM), jnp.int32)
    for doc in range(DOCS):
        value = jnp.where(sublanes((16, DIM)) < 8, counts[doc], clusters[doc])
        meta = jnp.where(doc_of_lane == doc, value, meta)
    block[BODY:BLOCK, :] = meta.astype(jnp.float32).astype(jnp.bfloat16)


def half_scores(rows, half, col_ref):
    first = half * 8
    blocks = rows.shape[0] // BODY
    best = None
    tops = [[] for _ in range(blocks)]
    for tile in range(8):
        keys = [
            col_ref[first : first + 8, (2 * tile + k) * 16 : (2 * tile + k + 1) * 16, :].reshape(
                128, DIM
            )
            for k in range(2)
        ]
        scores = lax.dot_general(
            rows,
            jnp.concatenate(keys, axis=0),
            (((1,), (1,)), ((), ())),
            preferred_element_type=jnp.float32,
        )
        for k in range(2):
            part = scores[:, 128 * k : 128 * (k + 1)]
            best = part if best is None else jnp.maximum(best, part)
            for q in range(blocks):
                block = part[BODY * q : BODY * (q + 1)]
                tops[q].append(jnp.max(block.reshape(BODY // 8, 8, 128), axis=0))
    return [best[BODY * q : BODY * (q + 1)] for q in range(blocks)], tops


def row_owner(r):
    x, y, z, core = position()
    xs = sum(offset[0] * 4**k for k, offset in enumerate(ROWS))
    ys = sum(offset[1] * 4**k for k, offset in enumerate(ROWS))
    return device_at((x + (xs >> (2 * r))) & 3, (y + (ys >> (2 * r))) & 3, z, core)


def kernel(
    quantized_hbm, scales_hbm, counts_hbm, clusters_hbm,
    best_ref,
    quantized, scales, counts, clusters, load_sem,
    stage, col_ref, row_ref, key_count, key_cluster, row_side, row_best, col_best, row_out, col_out, row_in, col_in,
    col_send, col_recv, core_send, core_recv, row_send, row_recv,
    col_out_send, col_in_recv, row_out_send, row_in_recv,
):
    loads = [
        pltpu.make_async_copy(source, target, load_sem.at[k])
        for k, (source, target) in enumerate(
            (
                (counts_hbm, counts),
                (clusters_hbm, clusters),
                (scales_hbm, scales),
                (quantized_hbm, quantized),
            )
        )
    ]
    for load in loads:
        load.start()
    barrier = pltpu.get_barrier_semaphore()
    around = partners()
    for offset, other in around:
        pl.semaphore_signal(barrier, 1, device_id=shifted(offset, other), device_id_type=MESH)
    for load in loads:
        load.wait()
    own = col_ref.at[0]
    prepare(quantized, scales, counts, clusters, stage, own)
    row_ref[0] = col_ref[0]
    col_best[...] = jnp.full(col_best.shape, NEG_FILL, jnp.float32)
    pl.semaphore_wait(barrier, len(around))

    def remote(source, target, send, recv, device):
        return pltpu.make_async_remote_copy(
            src_ref=source,
            dst_ref=target,
            send_sem=send,
            recv_sem=recv,
            device_id=device,
            device_id_type=MESH,
        )

    def along(k, source, target, part, device):
        source, target = col_ref.at[2 * source], col_ref.at[2 * target]
        if part is not None:
            source, target = source.at[part[0] : part[1]], target.at[part[0] : part[1]]
        return remote(source, target, col_send.at[k], col_recv.at[k], device)

    col_copies = [
        along(0, 4, 7, (CUT, BLOCK), shifted(COLS[3])),
        along(1, 0, 1, None, shifted(COLS[2])),
        along(2, 0, 2, None, shifted(COLS[1])),
        along(3, 0, 3, None, shifted(COLS[4])),
        along(4, 0, 4, None, shifted(COLS[3])),
        along(5, 3, 5, None, shifted(COLS[2])),
        along(6, 4, 6, None, shifted(COLS[1])),
        along(7, 3, 7, (0, CUT), shifted(COLS[4])),
    ]
    core_copies = [
        remote(
            col_ref.at[2 * k],
            col_ref.at[2 * k + 1],
            core_send.at[k],
            core_recv.at[k],
            shifted((0, 0, 0), 1),
        )
        for k in range(N_COLS)
    ]
    row_copies = [
        remote(own, row_ref.at[r], row_send.at[r], row_recv.at[r], shifted(ROWS[r], 0, -1))
        for r in range(1, N_ROWS)
    ]
    for k in (3, 4, 1, 2):
        col_copies[k].start()
    core_copies[0].start()
    row_waves = ((1, 2, 3), (4, 5, 6), (7, 8, 9))
    for k, wave in enumerate(row_waves):
        for r in row_waves[k - 1] if k else ():
            row_copies[r - 1].wait_send()
        for r in wave:
            row_copies[r - 1].start()
    col_copies[3].wait_recv()
    col_copies[5].start()
    col_copies[7].start()
    col_copies[4].wait_recv()
    col_copies[6].start()
    col_copies[0].start()
    core_copies[3].start()
    for k in (1, 2):
        col_copies[k].wait_recv()
        core_copies[k].start()
    core_copies[4].start()

    small = (8, DIM)
    lane = lanes(small)
    sub = sublanes(small)
    factor = 0.5 / math.sqrt(DIM)
    same_doc = (lane % DOCS) == (sub % DOCS)

    def read_meta(half):
        for k in range(4 * half, 4 * half + 4):
            core_copies[k].wait_recv()
        meta = jnp.zeros((16, DIM), jnp.float32)
        for k in range(8):
            part = col_ref[8 * half + k, BODY:BLOCK, :].astype(jnp.float32)
            meta = jnp.where(lanes((16, DIM)) // 16 == k, part, meta)
        key_count[half] = meta[0:8]
        key_cluster[half] = meta[8:16]

    def row_meta(r):
        meta = row_ref[r, BODY:BLOCK, :].astype(jnp.float32)
        pick = lanes((16, DIM)) == sublanes((16, DIM)) % DOCS
        chosen = jnp.sum(jnp.where(pick, meta, 0.0), axis=1, keepdims=True)
        row_side[r, 0] = jnp.broadcast_to(chosen[0:8], small)
        row_side[r, 1] = jnp.broadcast_to(chosen[8:16], small)

    def pair_unit(p, half):
        rows = row_ref[pl.ds(2 * p, 2), 0:BODY, :].reshape(2 * BODY, DIM)
        bests, all_tops = half_scores(rows, half, col_ref)
        found = []
        for q in range(2):
            r = 2 * p + q
            row_count, row_cluster = row_side[r, 0], row_side[r, 1]
            best = roll_max(bests[q], (DIM - 4, DIM - 8), 1)
            forward = roll_sum(jnp.sum(best.reshape(BODY // 8, 8, DIM), axis=0), (4,), 0)
            start = jnp.where(sub < 4, best[0:8], pltpu.roll(best[0:8], 4, 0))
            forward = forward - (TOKS - row_count) * start
            tops = [roll_max(top, (4,), 0) for top in all_tops[q]]
            backward = roll_sum(functools.reduce(jnp.add, tops), (DIM - 4, DIM - 8), 1)
            backward = backward - (TOKS - key_count[half]) * tops[0]
            chamfer = factor * (forward / row_count + backward / key_count[half])
            distinct = lane % 16 < DOCS
            if half == 0:
                distinct = distinct & ~((lane // 16 == 0) & same_doc & (r == 0))
            partner = distinct & (key_cluster[half] == row_cluster)
            found.append((jnp.where(distinct, chamfer, NEG_FILL), jnp.where(partner, chamfer, NEG_FILL)))
        for side in range(2):
            top = jnp.maximum(found[0][side], found[1][side])
            col_best[half, side] = jnp.maximum(col_best[half, side], top)
        return found

    def row_copy(r):
        return remote(row_ref.at[0], row_ref.at[r], row_send.at[r], row_recv.at[r], row_owner(r))

    def row_result(r):
        return remote(
            row_out.at[r], row_in.at[r], row_out_send.at[r], row_in_recv.at[r], row_owner(r)
        )

    def first_half(p, state):
        @pl.when(p > 0)
        def _():
            row_copy(2 * p).wait_recv()

        row_copy(2 * p + 1).wait_recv()
        for q in range(2):
            row_meta(2 * p + q)
        for q, found in enumerate(pair_unit(p, 0)):
            row_best[2 * p + q, 0] = found[0]
            row_best[2 * p + q, 1] = found[1]
        return state

    def by_lane(value):
        top = jnp.broadcast_to(jnp.max(value, axis=1, keepdims=True), small)
        return roll_max(jnp.where(same_doc, top, NEG_FILL), (1, 2), 0)

    def second_half(p, state):
        for q, (overall, within) in enumerate(pair_unit(p, 1)):
            r = 2 * p + q
            overall = by_lane(jnp.maximum(overall, row_best[r, 0]))
            within = by_lane(jnp.maximum(within, row_best[r, 1]))
            row_out[r] = jnp.where(sub < 4, overall, within)

        return state

    col_outs = [
        remote(
            col_out.at[slot // 8],
            col_in.at[slot],
            col_out_send.at[slot],
            col_in_recv.at[slot],
            shifted(COLS[slot // 2], slot % 2),
        )
        for slot in range(SLOTS)
    ]

    def return_cols(half):
        overall = roll_max(col_best[half, 0], (4, 2, 1), 0)
        within = roll_max(col_best[half, 1], (4, 2, 1), 0)
        col_out[half] = jnp.where(sub < 4, overall, within)
        for slot in reversed(range(max(1, 8 * half), 8 * half + 8)):
            col_outs[slot].start()

    read_meta(0)
    lax.fori_loop(0, EARLY, first_half, 0)
    for k in (5, 6):
        col_copies[k].wait_recv()
        core_copies[k].start()
    col_copies[7].wait_recv()
    col_copies[0].wait_recv()
    core_copies[7].start()
    lax.fori_loop(EARLY, N_ROWS // 2, first_half, 0)
    return_cols(0)
    read_meta(1)
    lax.fori_loop(0, N_ROWS // 2, second_half, 0, unroll=True)
    return_cols(1)
    for r in reversed(range(1, N_ROWS)):
        row_result(r).start()

    for copy in col_copies + [row_copies[r - 1] for r in row_waves[-1]] + core_copies:
        copy.wait_send()
    total = jnp.where(lane // 16 == 0, col_out[0], NEG_FILL)
    for slot in range(1, SLOTS):
        col_outs[slot].wait_recv()
        total = jnp.maximum(total, jnp.where(lane // 16 == slot % 8, col_in[slot], NEG_FILL))
    total = roll_max(total, (16, 32, 64), 1)
    total = jnp.maximum(total, row_out[0])
    for r in range(1, N_ROWS):
        row_result(r).wait_recv()
        total = jnp.maximum(total, row_in[r])
    best_ref[...] = total
    for slot in range(1, SLOTS):
        col_outs[slot].wait_send()
    for r in range(1, N_ROWS):
        row_result(r).wait_send()


def shards(quantized, block_scales, token_counts, cluster_ids):
    vmem = pl.BlockSpec(memory_space=pltpu.VMEM)
    hbm = pl.BlockSpec(memory_space=pltpu.HBM)
    scores = pl.pallas_call(
        kernel,
        out_shape=jax.ShapeDtypeStruct((8, DIM), jnp.float32),
        in_specs=[hbm] * 4,
        out_specs=vmem,
        scratch_shapes=[
            pltpu.VMEM((DOCS, TOKS, DIM), jnp.bfloat16),
            pltpu.VMEM((DOCS, 4, TOKS), jnp.bfloat16),
            pltpu.SMEM((DOCS,), jnp.int32),
            pltpu.SMEM((DOCS,), jnp.int32),
            pltpu.SemaphoreType.DMA((4,)),
            pltpu.VMEM((BODY, DIM), jnp.float32),
            pltpu.VMEM((SLOTS, BLOCK, DIM), jnp.bfloat16),
            pltpu.VMEM((N_ROWS, BLOCK, DIM), jnp.bfloat16),
            pltpu.VMEM((2, 8, DIM), jnp.float32),
            pltpu.VMEM((2, 8, DIM), jnp.float32),
            pltpu.VMEM((N_ROWS, 2, 8, DIM), jnp.float32),
            pltpu.VMEM((N_ROWS, 2, 8, DIM), jnp.float32),
            pltpu.VMEM((2, 2, 8, DIM), jnp.float32),
            pltpu.VMEM((N_ROWS, 8, DIM), jnp.float32),
            pltpu.VMEM((2, 8, DIM), jnp.float32),
            pltpu.VMEM((N_ROWS, 8, DIM), jnp.float32),
            pltpu.VMEM((SLOTS, 8, DIM), jnp.float32),
            pltpu.SemaphoreType.DMA((N_COLS,)),
            pltpu.SemaphoreType.DMA((N_COLS,)),
            pltpu.SemaphoreType.DMA((N_COLS,)),
            pltpu.SemaphoreType.DMA((N_COLS,)),
            pltpu.SemaphoreType.DMA((N_ROWS,)),
            pltpu.SemaphoreType.DMA((N_ROWS,)),
            pltpu.SemaphoreType.DMA((SLOTS,)),
            pltpu.SemaphoreType.DMA((SLOTS,)),
            pltpu.SemaphoreType.DMA((N_ROWS,)),
            pltpu.SemaphoreType.DMA((N_ROWS,)),
        ],
        compiler_params=pltpu.CompilerParams(
            collective_id=0, has_side_effects=True, vmem_limit_bytes=63 << 20
        ),
    )(quantized, jnp.swapaxes(block_scales, 1, 2), token_counts, cluster_ids)
    return scores[0, :DOCS], scores[4, :DOCS]


def solution(mesh):
    placed = (
        P(("blk", "group"), None, None),
        P(("blk", "group"), None, None),
        P(("blk", "group")),
        P(("blk", "group")),
    )
    return jax.shard_map(
        shards,
        mesh=mesh,
        in_specs=placed,
        out_specs=(P(("blk", "group")), P(("blk", "group"))),
        check_vma=False,
    )
```

```python
import functools
import math

import jax
import jax.numpy as jnp
from jax import lax
from jax.experimental import pallas as pl
from jax.experimental.pallas import tpu as pltpu
from jax.sharding import PartitionSpec as P

NEG_FILL = -1e30
MESH = pl.DeviceIdType.MESH
TORUS = (4, 4, 8)

COLS = ((0, 0, 0), (0, 0, 1), (0, 0, 7), (0, 0, 2), (0, 0, 6), (0, 0, 3), (0, 0, 5), (0, 0, 4))
ROWS = (
    (0, 0, 0), (2, 0, 0), (1, 0, 0), (0, 1, 0), (3, 3, 0),
    (3, 1, 0), (1, 2, 0), (2, 3, 0), (0, 2, 0), (2, 2, 0),
)
FOLDED = (0, 4)
N_COLS = len(COLS)
N_ROWS = len(ROWS)
SLOTS = 2 * N_COLS
DOCS = 4
TOKS = 64
DIM = 128
BODY = DOCS * TOKS
BLOCK = BODY + 16
CUT = 144


def position():
    blk = lax.axis_index("blk")
    group = lax.axis_index("group")
    return group >> 1, (blk & 2) | (group & 1), blk >> 2, blk & 1


def device_at(x, y, z, core):
    return ((z << 2) | (y & 2) | core, (x << 1) | (y & 1))


def shifted(offset, other=0, sign=1):
    x, y, z, core = position()
    step = tuple(sign * v % n for v, n in zip(offset, TORUS))
    return device_at(
        (x + step[0]) & (TORUS[0] - 1) if step[0] else x,
        (y + step[1]) & (TORUS[1] - 1) if step[1] else y,
        (z + step[2]) & (TORUS[2] - 1) if step[2] else z,
        core ^ other if other else core,
    )


def partners():
    sends = set()
    for offset in COLS:
        minus = tuple(-v % n for v, n in zip(offset, TORUS))
        for other in (0, 1):
            sends.add((offset, other))
        sends.add((minus, 0))
    for offset in ROWS:
        minus = tuple(-v % n for v, n in zip(offset, TORUS))
        sends.add((offset, 0))
        sends.add((minus, 0))
    sends.discard(((0, 0, 0), 0))
    return sorted(sends)


def lanes(shape):
    return lax.broadcasted_iota(jnp.int32, shape, len(shape) - 1)


def sublanes(shape):
    return lax.broadcasted_iota(jnp.int32, shape, len(shape) - 2)


def roll_max(value, shifts, axis):
    for shift in shifts:
        value = jnp.maximum(value, pltpu.roll(value, shift, axis))
    return value


def roll_sum(value, shifts, axis):
    for shift in shifts:
        value = value + pltpu.roll(value, shift, axis)
    return value


def prepare(quantized, scales, counts, clusters, stage, block):
    tile = (TOKS, DIM)
    spread = (lanes((4, DIM)) // 32 == sublanes((4, DIM))).astype(jnp.bfloat16)
    token = sublanes(tile)
    for doc in range(DOCS):
        scale = lax.dot_general(
            scales[doc], spread, (((0,), (0,)), ((), ())), preferred_element_type=jnp.float32
        )
        value = quantized[doc].astype(jnp.float32) * scale
        value = value.astype(jnp.bfloat16).astype(jnp.float32)
        first = jnp.broadcast_to(value[0:1], tile)
        stage[pl.ds(doc, TOKS, stride=DOCS), :] = jnp.where(token < counts[doc], value, first)
    block[0:BODY, :] = stage[...].astype(jnp.bfloat16)
    doc_of_lane = lanes((16, DIM)) % DOCS
    meta = jnp.zeros((16, DIM), jnp.int32)
    for doc in range(DOCS):
        value = jnp.where(sublanes((16, DIM)) < 8, counts[doc], clusters[doc])
        meta = jnp.where(doc_of_lane == doc, value, meta)
    block[BODY:BLOCK, :] = meta.astype(jnp.float32).astype(jnp.bfloat16)


def half_scores(rows, half, folded, col_ref):
    first = half * 8
    blocks = rows.shape[0] // BODY
    best = None
    tops = [[] for _ in range(blocks)]
    if folded:
        pieces = [
            [(chip, 2 * part + odd) for chip in (first + 2, first + 6) for odd in (1, 0)]
            for part in range(8)
        ]
    else:
        pieces = [[(first, part)] for part in range(16)]
    width = 2 if folded else 8
    for tile in range(len(pieces) // 2):
        keys = [
            col_ref[slot : slot + width, 16 * t : 16 * t + 16, :].reshape(16 * width, DIM)
            for slot, t in pieces[2 * tile] + pieces[2 * tile + 1]
        ]
        scores = lax.dot_general(
            rows,
            jnp.concatenate(keys, axis=0),
            (((1,), (1,)), ((), ())),
            preferred_element_type=jnp.float32,
        )
        for k in range(2):
            part = scores[:, 128 * k : 128 * (k + 1)]
            best = part if best is None else jnp.maximum(best, part)
            for q in range(blocks):
                block = part[BODY * q : BODY * (q + 1)]
                tops[q].append(jnp.max(block.reshape(BODY // 8, 8, 128), axis=0))
    return [best[BODY * q : BODY * (q + 1)] for q in range(blocks)], tops


def row_owner(r):
    x, y, z, core = position()
    xs = sum(offset[0] * 4**k for k, offset in enumerate(ROWS))
    ys = sum(offset[1] * 4**k for k, offset in enumerate(ROWS))
    return device_at((x + (xs >> (2 * r))) & 3, (y + (ys >> (2 * r))) & 3, z, core)


def kernel(
    quantized_hbm, scales_hbm, counts_hbm, clusters_hbm,
    best_ref,
    quantized, scales, counts, clusters, load_sem,
    stage, col_ref, row_ref, key_count, key_cluster, row_side, row_best, col_best, row_out, col_out, row_in, col_in,
    col_send, col_recv, core_send, core_recv, row_send, row_recv,
    col_out_send, col_in_recv, row_out_send, row_in_recv,
):
    loads = [
        pltpu.make_async_copy(source, target, load_sem.at[k])
        for k, (source, target) in enumerate(
            (
                (counts_hbm, counts),
                (clusters_hbm, clusters),
                (scales_hbm, scales),
                (quantized_hbm, quantized),
            )
        )
    ]
    for load in loads:
        load.start()
    barrier = pltpu.get_barrier_semaphore()
    around = partners()
    for offset, other in around:
        pl.semaphore_signal(barrier, 1, device_id=shifted(offset, other), device_id_type=MESH)
    for load in loads:
        load.wait()
    own = col_ref.at[0]
    prepare(quantized, scales, counts, clusters, stage, own)
    row_ref[0] = col_ref[0]
    col_best[...] = jnp.full(col_best.shape, NEG_FILL, jnp.float32)
    pl.semaphore_wait(barrier, len(around))

    def remote(source, target, send, recv, device):
        return pltpu.make_async_remote_copy(
            src_ref=source,
            dst_ref=target,
            send_sem=send,
            recv_sem=recv,
            device_id=device,
            device_id_type=MESH,
        )

    def along(k, source, target, part, device):
        source, target = col_ref.at[2 * source], col_ref.at[2 * target]
        if part is not None:
            source, target = source.at[part[0] : part[1]], target.at[part[0] : part[1]]
        return remote(source, target, col_send.at[k], col_recv.at[k], device)

    col_copies = [
        along(0, 4, 7, (CUT, BLOCK), shifted(COLS[3])),
        along(1, 0, 1, None, shifted(COLS[2])),
        along(2, 0, 2, None, shifted(COLS[1])),
        along(3, 0, 3, None, shifted(COLS[4])),
        along(4, 0, 4, None, shifted(COLS[3])),
        along(5, 3, 5, None, shifted(COLS[2])),
        along(6, 4, 6, None, shifted(COLS[1])),
        along(7, 3, 7, (0, CUT), shifted(COLS[4])),
    ]
    core_copies = [
        remote(
            col_ref.at[2 * k],
            col_ref.at[2 * k + 1],
            core_send.at[k],
            core_recv.at[k],
            shifted((0, 0, 0), 1),
        )
        for k in range(N_COLS)
    ]
    row_copies = [
        remote(own, row_ref.at[r], row_send.at[r], row_recv.at[r], shifted(ROWS[r], 0, -1))
        for r in range(1, N_ROWS)
    ]
    for k in (3, 4, 1, 2):
        col_copies[k].start()
    core_copies[0].start()
    row_waves = (tuple(range(1, 10)),)
    for k, wave in enumerate(row_waves):
        for r in row_waves[k - 1] if k else ():
            row_copies[r - 1].wait_send()
        for r in wave:
            row_copies[r - 1].start()
    col_copies[3].wait_recv()
    col_copies[5].start()
    col_copies[7].start()
    col_copies[4].wait_recv()
    col_copies[6].start()
    col_copies[0].start()
    core_copies[3].start()
    for k in (1, 2):
        col_copies[k].wait_recv()
        core_copies[k].start()
    core_copies[4].start()

    small = (8, DIM)
    lane = lanes(small)
    sub = sublanes(small)
    factor = 0.5 / math.sqrt(DIM)
    same_doc = (lane % DOCS) == (sub % DOCS)

    def read_meta(half):
        for k in range(4 * half, 4 * half + 4):
            core_copies[k].wait_recv()
        meta = jnp.zeros((16, DIM), jnp.float32)
        for k in range(8):
            part = col_ref[8 * half + k, BODY:BLOCK, :].astype(jnp.float32)
            meta = jnp.where(lanes((16, DIM)) // 16 == k, part, meta)
        key_count[half] = meta[0:8]
        key_cluster[half] = meta[8:16]

    def row_meta(r):
        meta = row_ref[r, BODY:BLOCK, :].astype(jnp.float32)
        pick = lanes((16, DIM)) == sublanes((16, DIM)) % DOCS
        chosen = jnp.sum(jnp.where(pick, meta, 0.0), axis=1, keepdims=True)
        row_side[r, 0] = jnp.broadcast_to(chosen[0:8], small)
        row_side[r, 1] = jnp.broadcast_to(chosen[8:16], small)

    def pair_unit(p, half, folded=False):
        rows = row_ref[pl.ds(2 * p, 2), 0:BODY, :].reshape(2 * BODY, DIM)
        bests, all_tops = half_scores(rows, half, folded, col_ref)
        found = []
        for q in range(2):
            r = 2 * p + q
            row_count, row_cluster = row_side[r, 0], row_side[r, 1]
            best = roll_max(bests[q], ((32,) if folded else ()) + (DIM - 4, DIM - 8), 1)
            forward = roll_sum(jnp.sum(best.reshape(BODY // 8, 8, DIM), axis=0), (4,), 0)
            start = jnp.where(sub < 4, best[0:8], pltpu.roll(best[0:8], 4, 0))
            forward = forward - (TOKS - row_count) * start
            tops = [roll_max(top, (4,), 0) for top in all_tops[q]]
            backward = roll_sum(
                functools.reduce(jnp.add, tops),
                ((32,) if folded else ()) + (DIM - 4, DIM - 8),
                1,
            )
            backward = backward - (TOKS - key_count[half]) * tops[0]
            chamfer = factor * (forward / row_count + backward / key_count[half])
            distinct = lane % 16 < DOCS
            if folded:
                distinct = distinct & (lane // 32 % 2 == 1)
            if half == 0:
                distinct = distinct & ~((lane // 16 == 0) & same_doc & (r == 0))
            partner = distinct & (key_cluster[half] == row_cluster)
            found.append((jnp.where(distinct, chamfer, NEG_FILL), jnp.where(partner, chamfer, NEG_FILL)))
        for side in range(2):
            top = jnp.maximum(found[0][side], found[1][side])
            col_best[half, side] = jnp.maximum(col_best[half, side], top)
        return found

    def row_result(r):
        return remote(
            row_out.at[r], row_in.at[r], row_out_send.at[r], row_in_recv.at[r], row_owner(r)
        )

    def first_half(pairs):
        members = [2 * p + q for p in pairs for q in range(2)]
        for r in members:
            if r:
                row_copies[r - 1].wait_recv()
        for r in members:
            row_meta(r)
        for p in pairs:
            for q, found in enumerate(pair_unit(p, 0)):
                row_best[2 * p + q, 0] = found[0]
                row_best[2 * p + q, 1] = found[1]

    def by_lane(value):
        top = jnp.broadcast_to(jnp.max(value, axis=1, keepdims=True), small)
        return roll_max(jnp.where(same_doc, top, NEG_FILL), (1, 2), 0)

    def second_half(p):
        for q, (overall, within) in enumerate(pair_unit(p, 1, p in FOLDED)):
            r = 2 * p + q
            overall = by_lane(jnp.maximum(overall, row_best[r, 0]))
            within = by_lane(jnp.maximum(within, row_best[r, 1]))
            row_out[r] = jnp.where(sub < 4, overall, within)


    col_outs = [
        remote(
            col_out.at[slot // 8],
            col_in.at[slot],
            col_out_send.at[slot],
            col_in_recv.at[slot],
            shifted(COLS[slot // 2], slot % 2),
        )
        for slot in range(SLOTS)
    ]

    def return_cols(half):
        overall = roll_max(col_best[half, 0], (4, 2, 1), 0)
        within = roll_max(col_best[half, 1], (4, 2, 1), 0)
        col_out[half] = jnp.where(sub < 4, overall, within)
        for slot in reversed(range(max(1, 8 * half), 8 * half + 8)):
            col_outs[slot].start()

    read_meta(0)
    first_half((0, 1))
    first_half((2, 3))
    for k in (5, 6):
        col_copies[k].wait_recv()
        core_copies[k].start()
    col_copies[7].wait_recv()
    col_copies[0].wait_recv()
    core_copies[7].start()
    first_half((4,))
    return_cols(0)
    read_meta(1)
    for p in range(N_ROWS // 2):
        second_half(p)
    return_cols(1)
    for r in reversed(range(1, N_ROWS)):
        row_result(r).start()

    for copy in col_copies + [row_copies[r - 1] for r in row_waves[-1]] + core_copies:
        copy.wait_send()
    total = jnp.where(lane // 16 == 0, col_out[0], NEG_FILL)
    for slot in range(1, SLOTS):
        col_outs[slot].wait_recv()
        total = jnp.maximum(total, jnp.where(lane // 16 == slot % 8, col_in[slot], NEG_FILL))
    total = roll_max(total, (16, 32, 64), 1)
    total = jnp.maximum(total, row_out[0])
    for r in range(1, N_ROWS):
        row_result(r).wait_recv()
        total = jnp.maximum(total, row_in[r])
    best_ref[...] = total
    for slot in range(1, SLOTS):
        col_outs[slot].wait_send()
    for r in range(1, N_ROWS):
        row_result(r).wait_send()


def shards(quantized, block_scales, token_counts, cluster_ids):
    vmem = pl.BlockSpec(memory_space=pltpu.VMEM)
    hbm = pl.BlockSpec(memory_space=pltpu.HBM)
    scores = pl.pallas_call(
        kernel,
        out_shape=jax.ShapeDtypeStruct((8, DIM), jnp.float32),
        in_specs=[hbm] * 4,
        out_specs=vmem,
        scratch_shapes=[
            pltpu.VMEM((DOCS, TOKS, DIM), jnp.bfloat16),
            pltpu.VMEM((DOCS, 4, TOKS), jnp.bfloat16),
            pltpu.SMEM((DOCS,), jnp.int32),
            pltpu.SMEM((DOCS,), jnp.int32),
            pltpu.SemaphoreType.DMA((4,)),
            pltpu.VMEM((BODY, DIM), jnp.float32),
            pltpu.VMEM((SLOTS, BLOCK, DIM), jnp.bfloat16),
            pltpu.VMEM((N_ROWS, BLOCK, DIM), jnp.bfloat16),
            pltpu.VMEM((2, 8, DIM), jnp.float32),
            pltpu.VMEM((2, 8, DIM), jnp.float32),
            pltpu.VMEM((N_ROWS, 2, 8, DIM), jnp.float32),
            pltpu.VMEM((N_ROWS, 2, 8, DIM), jnp.float32),
            pltpu.VMEM((2, 2, 8, DIM), jnp.float32),
            pltpu.VMEM((N_ROWS, 8, DIM), jnp.float32),
            pltpu.VMEM((2, 8, DIM), jnp.float32),
            pltpu.VMEM((N_ROWS, 8, DIM), jnp.float32),
            pltpu.VMEM((SLOTS, 8, DIM), jnp.float32),
            pltpu.SemaphoreType.DMA((N_COLS,)),
            pltpu.SemaphoreType.DMA((N_COLS,)),
            pltpu.SemaphoreType.DMA((N_COLS,)),
            pltpu.SemaphoreType.DMA((N_COLS,)),
            pltpu.SemaphoreType.DMA((N_ROWS,)),
            pltpu.SemaphoreType.DMA((N_ROWS,)),
            pltpu.SemaphoreType.DMA((SLOTS,)),
            pltpu.SemaphoreType.DMA((SLOTS,)),
            pltpu.SemaphoreType.DMA((N_ROWS,)),
            pltpu.SemaphoreType.DMA((N_ROWS,)),
        ],
        compiler_params=pltpu.CompilerParams(
            collective_id=0, has_side_effects=True, vmem_limit_bytes=63 << 20
        ),
    )(quantized, jnp.swapaxes(block_scales, 1, 2), token_counts, cluster_ids)
    return scores[0, :DOCS], scores[4, :DOCS]


def solution(mesh):
    placed = (
        P(("blk", "group"), None, None),
        P(("blk", "group"), None, None),
        P(("blk", "group")),
        P(("blk", "group")),
    )
    return jax.shard_map(
        shards,
        mesh=mesh,
        in_specs=placed,
        out_specs=(P(("blk", "group")), P(("blk", "group"))),
        check_vma=False,
    )
```

```python
import functools
import math

import jax
import jax.numpy as jnp
from jax import lax
from jax.experimental import pallas as pl
from jax.experimental.pallas import tpu as pltpu
from jax.sharding import PartitionSpec as P

NEG_FILL = -1e30
MESH = pl.DeviceIdType.MESH
TORUS = (4, 4, 8)

COLS = ((0, 0, 0), (0, 0, 1), (0, 0, 7), (0, 0, 2), (0, 0, 6), (0, 0, 3), (0, 0, 5), (0, 0, 4))
ROWS = (
    (0, 0, 0), (2, 0, 0), (1, 0, 0), (0, 1, 0), (3, 3, 0),
    (3, 1, 0), (1, 2, 0), (2, 3, 0), (0, 2, 0), (2, 2, 0),
)
FOLDED = (0, 4)
N_COLS = len(COLS)
N_ROWS = len(ROWS)
SLOTS = 2 * N_COLS
DOCS = 4
TOKS = 64
DIM = 128
BODY = DOCS * TOKS
BLOCK = BODY + 16
CUT = 144


def position():
    blk = lax.axis_index("blk")
    group = lax.axis_index("group")
    return group >> 1, (blk & 2) | (group & 1), blk >> 2, blk & 1


def device_at(x, y, z, core):
    return ((z << 2) | (y & 2) | core, (x << 1) | (y & 1))


def shifted(offset, other=0, sign=1):
    x, y, z, core = position()
    step = tuple(sign * v % n for v, n in zip(offset, TORUS))
    return device_at(
        (x + step[0]) & (TORUS[0] - 1) if step[0] else x,
        (y + step[1]) & (TORUS[1] - 1) if step[1] else y,
        (z + step[2]) & (TORUS[2] - 1) if step[2] else z,
        core ^ other if other else core,
    )


def partners():
    sends = set()
    for offset in COLS:
        minus = tuple(-v % n for v, n in zip(offset, TORUS))
        for other in (0, 1):
            sends.add((offset, other))
        sends.add((minus, 0))
    for offset in ROWS:
        minus = tuple(-v % n for v, n in zip(offset, TORUS))
        sends.add((offset, 0))
        sends.add((minus, 0))
    sends.discard(((0, 0, 0), 0))
    return sorted(sends)


def lanes(shape):
    return lax.broadcasted_iota(jnp.int32, shape, len(shape) - 1)


def sublanes(shape):
    return lax.broadcasted_iota(jnp.int32, shape, len(shape) - 2)


def roll_max(value, shifts, axis):
    for shift in shifts:
        value = jnp.maximum(value, pltpu.roll(value, shift, axis))
    return value


def roll_sum(value, shifts, axis):
    for shift in shifts:
        value = value + pltpu.roll(value, shift, axis)
    return value


def prepare(quantized, scales, counts, clusters, stage, block):
    tile = (TOKS, DIM)
    spread = (lanes((4, DIM)) // 32 == sublanes((4, DIM))).astype(jnp.bfloat16)
    token = sublanes(tile)
    for doc in range(DOCS):
        scale = lax.dot_general(
            scales[doc], spread, (((0,), (0,)), ((), ())), preferred_element_type=jnp.float32
        )
        value = quantized[doc].astype(jnp.float32) * scale
        value = value.astype(jnp.bfloat16).astype(jnp.float32)
        first = jnp.broadcast_to(value[0:1], tile)
        stage[pl.ds(doc, TOKS, stride=DOCS), :] = jnp.where(token < counts[doc], value, first)
    block[0:BODY, :] = stage[...].astype(jnp.bfloat16)
    doc_of_lane = lanes((16, DIM)) % DOCS
    meta = jnp.zeros((16, DIM), jnp.int32)
    for doc in range(DOCS):
        value = jnp.where(sublanes((16, DIM)) < 8, counts[doc], clusters[doc])
        meta = jnp.where(doc_of_lane == doc, value, meta)
    block[BODY:BLOCK, :] = meta.astype(jnp.float32).astype(jnp.bfloat16)


def half_scores(rows, half, folded, col_ref):
    first = half * 8
    blocks = rows.shape[0] // BODY
    best = None
    tops = [[] for _ in range(blocks)]
    if folded:
        pieces = [
            [(chip, 2 * part + odd) for chip in (first + 2, first + 6) for odd in (1, 0)]
            for part in range(8)
        ]
    else:
        pieces = [[(first, part)] for part in range(16)]
    width = 2 if folded else 8
    for tile in range(len(pieces) // 2):
        keys = [
            col_ref[slot : slot + width, 16 * t : 16 * t + 16, :].reshape(16 * width, DIM)
            for slot, t in pieces[2 * tile] + pieces[2 * tile + 1]
        ]
        scores = lax.dot_general(
            rows,
            jnp.concatenate(keys, axis=0),
            (((1,), (1,)), ((), ())),
            preferred_element_type=jnp.float32,
        )
        for k in range(2):
            part = scores[:, 128 * k : 128 * (k + 1)]
            best = part if best is None else jnp.maximum(best, part)
            for q in range(blocks):
                block = part[BODY * q : BODY * (q + 1)]
                tops[q].append(jnp.max(block.reshape(BODY // 8, 8, 128), axis=0))
    return [best[BODY * q : BODY * (q + 1)] for q in range(blocks)], tops


def row_owner(r):
    x, y, z, core = position()
    xs = sum(offset[0] * 4**k for k, offset in enumerate(ROWS))
    ys = sum(offset[1] * 4**k for k, offset in enumerate(ROWS))
    return device_at((x + (xs >> (2 * r))) & 3, (y + (ys >> (2 * r))) & 3, z, core)


def kernel(
    quantized_hbm, scales_hbm, counts_hbm, clusters_hbm,
    best_ref,
    quantized, scales, counts, clusters, load_sem,
    stage, col_ref, row_ref, key_count, key_cluster, row_side, row_best, col_best, row_out, col_out, row_in, col_in,
    col_send, col_recv, core_send, core_recv, row_send, row_recv,
    col_out_send, col_in_recv, row_out_send, row_in_recv,
):
    loads = [
        pltpu.make_async_copy(source, target, load_sem.at[k])
        for k, (source, target) in enumerate(
            (
                (counts_hbm, counts),
                (clusters_hbm, clusters),
                (scales_hbm, scales),
                (quantized_hbm, quantized),
            )
        )
    ]
    for load in loads:
        load.start()
    barrier = pltpu.get_barrier_semaphore()
    around = partners()
    for offset, other in around:
        pl.semaphore_signal(barrier, 1, device_id=shifted(offset, other), device_id_type=MESH)
    for load in loads:
        load.wait()
    own = col_ref.at[0]
    prepare(quantized, scales, counts, clusters, stage, own)
    row_ref[0] = col_ref[0]
    col_best[...] = jnp.full(col_best.shape, NEG_FILL, jnp.float32)
    pl.semaphore_wait(barrier, len(around))

    def remote(source, target, send, recv, device):
        return pltpu.make_async_remote_copy(
            src_ref=source,
            dst_ref=target,
            send_sem=send,
            recv_sem=recv,
            device_id=device,
            device_id_type=MESH,
        )

    def along(k, source, target, part, device):
        source, target = col_ref.at[2 * source], col_ref.at[2 * target]
        if part is not None:
            source, target = source.at[part[0] : part[1]], target.at[part[0] : part[1]]
        return remote(source, target, col_send.at[k], col_recv.at[k], device)

    col_copies = [
        along(0, 4, 7, (CUT, BLOCK), shifted(COLS[3])),
        along(1, 0, 1, None, shifted(COLS[2])),
        along(2, 0, 2, None, shifted(COLS[1])),
        along(3, 0, 3, None, shifted(COLS[4])),
        along(4, 0, 4, None, shifted(COLS[3])),
        along(5, 3, 5, None, shifted(COLS[2])),
        along(6, 4, 6, None, shifted(COLS[1])),
        along(7, 3, 7, (0, CUT), shifted(COLS[4])),
    ]
    core_copies = [
        remote(
            col_ref.at[2 * k],
            col_ref.at[2 * k + 1],
            core_send.at[k],
            core_recv.at[k],
            shifted((0, 0, 0), 1),
        )
        for k in range(N_COLS)
    ]
    row_copies = [
        remote(own, row_ref.at[r], row_send.at[r], row_recv.at[r], shifted(ROWS[r], 0, -1))
        for r in range(1, N_ROWS)
    ]
    for k in (3, 4, 1, 2):
        col_copies[k].start()
    core_copies[0].start()
    row_waves = (tuple(range(1, 10)),)
    for k, wave in enumerate(row_waves):
        for r in row_waves[k - 1] if k else ():
            row_copies[r - 1].wait_send()
        for r in wave:
            row_copies[r - 1].start()
    col_copies[3].wait_recv()
    col_copies[5].start()
    col_copies[7].start()
    col_copies[4].wait_recv()
    col_copies[6].start()
    col_copies[0].start()
    core_copies[3].start()
    for k in (1, 2):
        col_copies[k].wait_recv()
        core_copies[k].start()
    core_copies[4].start()

    small = (8, DIM)
    lane = lanes(small)
    sub = sublanes(small)
    factor = 0.5 / math.sqrt(DIM)
    same_doc = (lane % DOCS) == (sub % DOCS)

    def read_meta(half):
        for k in range(4 * half, 4 * half + 4):
            core_copies[k].wait_recv()
        meta = jnp.zeros((16, DIM), jnp.float32)
        for k in range(8):
            part = col_ref[8 * half + k, BODY:BLOCK, :].astype(jnp.float32)
            meta = jnp.where(lanes((16, DIM)) // 16 == k, part, meta)
        key_count[half] = meta[0:8]
        key_cluster[half] = meta[8:16]

    def row_meta(r):
        meta = row_ref[r, BODY:BLOCK, :].astype(jnp.float32)
        pick = lanes((16, DIM)) == sublanes((16, DIM)) % DOCS
        chosen = jnp.sum(jnp.where(pick, meta, 0.0), axis=1, keepdims=True)
        row_side[r, 0] = jnp.broadcast_to(chosen[0:8], small)
        row_side[r, 1] = jnp.broadcast_to(chosen[8:16], small)

    def pair_unit(p, half, folded=False):
        rows = row_ref[pl.ds(2 * p, 2), 0:BODY, :].reshape(2 * BODY, DIM)
        bests, all_tops = half_scores(rows, half, folded, col_ref)
        found = []
        for q in range(2):
            r = 2 * p + q
            row_count, row_cluster = row_side[r, 0], row_side[r, 1]
            best = roll_max(bests[q], ((32,) if folded else ()) + (DIM - 4, DIM - 8), 1)
            forward = roll_sum(jnp.sum(best.reshape(BODY // 8, 8, DIM), axis=0), (4,), 0)
            start = jnp.where(sub < 4, best[0:8], pltpu.roll(best[0:8], 4, 0))
            forward = forward - (TOKS - row_count) * start
            tops = [roll_max(top, (4,), 0) for top in all_tops[q]]
            backward = roll_sum(
                functools.reduce(jnp.add, tops),
                ((32,) if folded else ()) + (DIM - 4, DIM - 8),
                1,
            )
            backward = backward - (TOKS - key_count[half]) * tops[0]
            chamfer = factor * (forward / row_count + backward / key_count[half])
            distinct = lane % 16 < DOCS
            if folded:
                distinct = distinct & (lane // 32 % 2 == 1)
            if half == 0:
                distinct = distinct & ~((lane // 16 == 0) & same_doc & (r == 0))
            partner = distinct & (key_cluster[half] == row_cluster)
            found.append((jnp.where(distinct, chamfer, NEG_FILL), jnp.where(partner, chamfer, NEG_FILL)))
        for side in range(2):
            top = jnp.maximum(found[0][side], found[1][side])
            col_best[half, side] = jnp.maximum(col_best[half, side], top)
        return found

    def row_result(r):
        return remote(
            row_out.at[r], row_in.at[r], row_out_send.at[r], row_in_recv.at[r], row_owner(r)
        )

    def first_half(pairs):
        members = [2 * p + q for p in pairs for q in range(2)]
        for r in members:
            if r:
                row_copies[r - 1].wait_recv()
        for r in members:
            row_meta(r)
        for p in pairs:
            for q, found in enumerate(pair_unit(p, 0)):
                row_best[2 * p + q, 0] = found[0]
                row_best[2 * p + q, 1] = found[1]

    def by_lane(value):
        top = jnp.broadcast_to(jnp.max(value, axis=1, keepdims=True), small)
        return roll_max(jnp.where(same_doc, top, NEG_FILL), (1, 2), 0)

    def second_half(p):
        for q, (overall, within) in enumerate(pair_unit(p, 1, p in FOLDED)):
            r = 2 * p + q
            overall = by_lane(jnp.maximum(overall, row_best[r, 0]))
            within = by_lane(jnp.maximum(within, row_best[r, 1]))
            row_out[r] = jnp.where(sub < 4, overall, within)


    col_outs = [
        remote(
            col_out.at[slot // 8],
            col_in.at[slot],
            col_out_send.at[slot],
            col_in_recv.at[slot],
            shifted(COLS[slot // 2], slot % 2),
        )
        for slot in range(SLOTS)
    ]

    def return_cols(half):
        overall = roll_max(col_best[half, 0], (4, 2, 1), 0)
        within = roll_max(col_best[half, 1], (4, 2, 1), 0)
        col_out[half] = jnp.where(sub < 4, overall, within)
        for slot in reversed(range(max(1, 8 * half), 8 * half + 8)):
            col_outs[slot].start()

    read_meta(0)
    first_half((0, 1))
    first_half((2, 3))
    for k in (5, 6):
        col_copies[k].wait_recv()
        core_copies[k].start()
    col_copies[7].wait_recv()
    col_copies[0].wait_recv()
    core_copies[7].start()
    first_half((4,))
    return_cols(0)
    read_meta(1)
    for p in range(N_ROWS // 2):
        second_half(p)
        if p == 2:
            for r in reversed(range(1, 6)):
                row_result(r).start()
    return_cols(1)
    for r in reversed(range(6, N_ROWS)):
        row_result(r).start()

    for copy in col_copies + [row_copies[r - 1] for r in row_waves[-1]] + core_copies:
        copy.wait_send()
    total = jnp.where(lane // 16 == 0, col_out[0], NEG_FILL)
    for slot in range(1, SLOTS):
        col_outs[slot].wait_recv()
        total = jnp.maximum(total, jnp.where(lane // 16 == slot % 8, col_in[slot], NEG_FILL))
    total = roll_max(total, (16, 32, 64), 1)
    total = jnp.maximum(total, row_out[0])
    for r in range(1, N_ROWS):
        row_result(r).wait_recv()
        total = jnp.maximum(total, row_in[r])
    best_ref[...] = total
    for slot in range(1, SLOTS):
        col_outs[slot].wait_send()
    for r in range(1, N_ROWS):
        row_result(r).wait_send()


def shards(quantized, block_scales, token_counts, cluster_ids):
    vmem = pl.BlockSpec(memory_space=pltpu.VMEM)
    hbm = pl.BlockSpec(memory_space=pltpu.HBM)
    scores = pl.pallas_call(
        kernel,
        out_shape=jax.ShapeDtypeStruct((8, DIM), jnp.float32),
        in_specs=[hbm] * 4,
        out_specs=vmem,
        scratch_shapes=[
            pltpu.VMEM((DOCS, TOKS, DIM), jnp.bfloat16),
            pltpu.VMEM((DOCS, 4, TOKS), jnp.bfloat16),
            pltpu.SMEM((DOCS,), jnp.int32),
            pltpu.SMEM((DOCS,), jnp.int32),
            pltpu.SemaphoreType.DMA((4,)),
            pltpu.VMEM((BODY, DIM), jnp.float32),
            pltpu.VMEM((SLOTS, BLOCK, DIM), jnp.bfloat16),
            pltpu.VMEM((N_ROWS, BLOCK, DIM), jnp.bfloat16),
            pltpu.VMEM((2, 8, DIM), jnp.float32),
            pltpu.VMEM((2, 8, DIM), jnp.float32),
            pltpu.VMEM((N_ROWS, 2, 8, DIM), jnp.float32),
            pltpu.VMEM((N_ROWS, 2, 8, DIM), jnp.float32),
            pltpu.VMEM((2, 2, 8, DIM), jnp.float32),
            pltpu.VMEM((N_ROWS, 8, DIM), jnp.float32),
            pltpu.VMEM((2, 8, DIM), jnp.float32),
            pltpu.VMEM((N_ROWS, 8, DIM), jnp.float32),
            pltpu.VMEM((SLOTS, 8, DIM), jnp.float32),
            pltpu.SemaphoreType.DMA((N_COLS,)),
            pltpu.SemaphoreType.DMA((N_COLS,)),
            pltpu.SemaphoreType.DMA((N_COLS,)),
            pltpu.SemaphoreType.DMA((N_COLS,)),
            pltpu.SemaphoreType.DMA((N_ROWS,)),
            pltpu.SemaphoreType.DMA((N_ROWS,)),
            pltpu.SemaphoreType.DMA((SLOTS,)),
            pltpu.SemaphoreType.DMA((SLOTS,)),
            pltpu.SemaphoreType.DMA((N_ROWS,)),
            pltpu.SemaphoreType.DMA((N_ROWS,)),
        ],
        compiler_params=pltpu.CompilerParams(
            collective_id=0, has_side_effects=True, vmem_limit_bytes=63 << 20
        ),
    )(quantized, jnp.swapaxes(block_scales, 1, 2), token_counts, cluster_ids)
    return scores[0, :DOCS], scores[4, :DOCS]


def solution(mesh):
    placed = (
        P(("blk", "group"), None, None),
        P(("blk", "group"), None, None),
        P(("blk", "group")),
        P(("blk", "group")),
    )
    return jax.shard_map(
        shards,
        mesh=mesh,
        in_specs=placed,
        out_specs=(P(("blk", "group")), P(("blk", "group"))),
        check_vma=False,
    )
```
